32 devices in a mesh: fold: 4 (over x, core), tile: 8 (over z, y).
Axes of the slice: x: 2, y: 2, z: 4, core: 2. Of those that a mesh axis runs over, the one named last changes fastest.
Arguments:
- design: bfloat16 [8192, 8192], P('fold', 'tile'), may hold values from -0.0625 to 0.0625
- weights: float32 [8192], P('fold'), may hold values from 0.2 to 5
- response: float32 [8192], P('fold'), may hold values from -6 to 6
- fold_of: int32 [32], P('fold'), may hold values from 0 to 7, as said below
- smoothing: float32 [128], P('tile'), may hold values from 0.05 to 1
Outputs:
- complement: float32 [8, 8192, 8192], P('fold', 'tile')
- complement_rhs: float32 [8, 8192], P('fold', 'tile')
The draws below stay inside these ranges and needn't reach their ends.
Inputs may be any that keep to these rules, and one draw needn't show every extreme that they name: `fold_of`: the slabs of rows g * 2048 to (g + 1) * 2048 - 1 carry only fold ids g * 2 to (g + 1) * 2 - 1, and each of these appears on at least one of those slabs.
All inputs are finite; a program needn't handle non-finite values.
Results may differ from the reference program's by a relative error of at most 0.0029.
Values may be sent and summed in bfloat16 or wider, within the bound.
A program may use at most 512 MiB of HBM per device.

```python
import math
import jax
import jax.numpy as jnp
from jax import lax

P_SIZE = 8192
FOLDS = 8
TERM = 64
SLAB = 256
ROWS_DEV = 2048
ROWS = 8192
TERMS = 128


def draw_fold_of(key, part):
    per_group = ROWS_DEV // SLAB
    groups = ROWS // ROWS_DEV
    per_fold = FOLDS // groups
    scores = jax.random.randint(jax.random.fold_in(key, 11), (groups, per_group), 0, 1 << 20).astype(jnp.int32)
    scores = scores * per_group + jnp.arange(per_group, dtype=jnp.int32)[None, :]
    ranks = jnp.argsort(jnp.argsort(scores, axis=1, stable=True), axis=1, stable=True).astype(jnp.int32)
    extra = jax.random.randint(jax.random.fold_in(key, 12), (groups, per_group), 0, per_fold).astype(jnp.int32)
    local_id = jnp.where(ranks < per_fold, ranks, extra)
    folds = jnp.arange(groups, dtype=jnp.int32)[:, None] * per_fold + local_id
    return folds.reshape(-1).astype(jnp.int32)


def shard_levels(rng, dims, pieces, low, largest):
    gain, own = 1.0, jax.random.fold_in(rng, 6)
    for position, parts in pieces:
        steps = jnp.exp(jax.random.uniform(jax.random.fold_in(own, position), (parts,), jnp.float32, low / len(pieces), largest / len(pieces)))
        gain = gain * jnp.repeat(steps, dims[position] // parts).reshape([-1 if axis == position else 1 for axis in range(len(dims))])
    return gain


def normal_values(rng, extent, deviation, most, shards=(), kind=jnp.bfloat16):
    entries = deviation * jax.random.normal(rng, extent, jnp.float32)
    if shards:
        entries = entries * shard_levels(rng, extent, shards, -0.22, 0.18)
    return jnp.clip(entries, -most, most).astype(kind)


def setup_inputs(seed: int = 0) -> dict:
    streams_of = jax.random.split(jax.random.key(seed), 6)
    return {
        "design": normal_values(streams_of[0], (ROWS, P_SIZE), ROWS ** -0.5, 0.0625, ((0, 4), (1, 8))),
        "weights": jnp.clip(jnp.exp(math.log(5.0) - 3.218876 * jax.random.uniform(streams_of[1], (ROWS,), jnp.float32) ** shard_levels(streams_of[1], (ROWS,), ((0, 4),), -0.2, 0.2)), 0.2, 5.0),
        "response": normal_values(streams_of[2], (ROWS,), 1.0, 6.0, ((0, 4),), jnp.float32),
        "fold_of": draw_fold_of(jax.random.fold_in(streams_of[5], 71), 0),
        "smoothing": jnp.clip(jnp.exp(math.log(1.0) - 2.9957323 * jax.random.uniform(streams_of[4], (TERMS,), jnp.float32) ** shard_levels(streams_of[4], (TERMS,), ((0, 8),), -0.2, 0.2)), 0.05, 1.0),
    }


def second_differences(width):
    rows = lax.broadcasted_iota(jnp.int32, (width - 2, width), 0)
    cols = lax.broadcasted_iota(jnp.int32, (width - 2, width), 1)
    diffs = jnp.where(cols == rows, 1.0, 0.0) + jnp.where(cols == rows + 1, -2.0, 0.0) + jnp.where(cols == rows + 2, 1.0, 0.0)
    diffs = diffs.astype(jnp.float32)
    return jnp.dot(diffs.T, diffs, precision=lax.Precision.HIGHEST, preferred_element_type=jnp.float32)

def reference(design, weights, response, fold_of, smoothing):
    root_w = jnp.sqrt(weights)
    rooted = (design.astype(jnp.float32) * root_w[:, None]).astype(jnp.bfloat16)
    target = root_w * response
    slabs = rooted.reshape(-1, SLAB, P_SIZE)
    target_slabs = target.reshape(-1, SLAB)

    def add_slab(carry, item):
        grams, rhs = carry
        block, tvec, fid = item
        gram = jnp.dot(block.T, block, preferred_element_type=jnp.float32)
        right = jnp.dot(tvec, block.astype(jnp.float32), precision=lax.Precision.HIGHEST, preferred_element_type=jnp.float32)
        return ((grams.at[fid].add(gram), rhs.at[fid].add(right)), None)
    start = (jnp.zeros((FOLDS, P_SIZE, P_SIZE), jnp.float32), jnp.zeros((FOLDS, P_SIZE), jnp.float32))
    (grams, rhs), _ = lax.scan(add_slab, start, (slabs, target_slabs, fold_of.astype(jnp.int32)))
    total = lax.optimization_barrier(jnp.sum(grams, axis=0))
    total_rhs = lax.optimization_barrier(jnp.sum(rhs, axis=0))
    penalty = jnp.kron(jnp.diag(smoothing), second_differences(TERM))
    complement = total[None] - grams + penalty[None]
    return (complement, total_rhs[None] - rhs)
```

```python
import functools

import jax
import jax.numpy as jnp
from jax import lax
from jax.experimental import pallas as pl
from jax.experimental.pallas import tpu as pltpu
from jax.sharding import PartitionSpec as P

FOLDS = 8
TERM = 64
MESH = pl.DeviceIdType.MESH
SLOTS = 4


def second_differences(width):
    rows = lax.broadcasted_iota(jnp.int32, (width - 2, width), 0)
    cols = lax.broadcasted_iota(jnp.int32, (width - 2, width), 1)
    diffs = (
        jnp.where(cols == rows, 1.0, 0.0)
        + jnp.where(cols == rows + 1, -2.0, 0.0)
        + jnp.where(cols == rows + 2, 1.0, 0.0)
    )
    diffs = diffs.astype(jnp.float32)
    return jnp.dot(
        diffs.T, diffs, precision=lax.Precision.HIGHEST, preferred_element_type=jnp.float32
    )


def kernel(
    tiles, x_ref, mask_ref, target_ref, pen_ref, out_ref, crhs_ref,
    g, left, left_a, grams, rs_send, rs_recv, x_send, x_recv, ag_send, ag_recv,
    rhs, rhs_recv,
    in_sem, ring_send, ring_recv, rs_ss, rs_rs, x_ss, x_rs, ag_ss, ag_rs, out_sem,
    rhs_ss, rhs_rs,
):
    units = 2 * tiles
    depth, wide = g.shape[1], g.shape[2]
    block = 2 * wide
    half = block // 2
    sub_rows = depth // 2
    me = lax.axis_index("tile")
    fold = lax.axis_index("fold")
    core = fold % 2
    mate = fold + 1 - 2 * core
    across = (fold + 2) % 4
    place = (1 - me % 2) * (me // 2) + (me % 2) * (tiles - 1 - me // 2)

    def tile_at(position):
        position = position % tiles
        up = (position < tiles // 2).astype(jnp.int32)
        return up * (2 * position) + (1 - up) * (2 * (tiles - 1 - position) + 1)

    right = tile_at(place + 1)
    left_tile = tile_at(place + tiles - 1)
    neighbours = (right, left_tile)

    barrier = pltpu.get_barrier_semaphore()
    for device in ({"tile": right}, {"tile": left_tile}, {"fold": mate}, {"fold": across}):
        pl.semaphore_signal(barrier, inc=1, device_id=device, device_id_type=MESH)

    def load(side):
        return pltpu.make_async_copy(
            x_ref.at[:, pl.ds(side * wide, wide)], g.at[side], in_sem.at[side]
        )

    load(0).start()
    load(1).start()
    pl.semaphore_wait(barrier, 4)

    def hop(step, side, sub):
        rows = pl.ds(pl.multiple_of(sub * sub_rows, sub_rows), sub_rows)
        source, there = 2 * step + side, 2 * step + 2 + side
        return pltpu.make_async_remote_copy(
            src_ref=g.at[source, rows],
            dst_ref=g.at[there, rows],
            send_sem=ring_send.at[source, sub],
            recv_sem=ring_recv.at[there, sub],
            device_id={"tile": neighbours[side]},
            device_id_type=MESH,
        )

    for side in range(2):
        load(side).wait()
        for sub in range(2):
            hop(0, side, sub).start()

    chunk = 256
    for side in range(2):
        @pl.loop(0, depth // chunk)
        def _(i):
            at = pl.multiple_of(i * chunk, chunk)
            turned = g[side, pl.ds(at, chunk), :].T
            left[side * wide:(side + 1) * wide, pl.ds(at, chunk)] = turned
            kept = turned.astype(jnp.float32) * mask_ref[:, pl.ds(at, chunk)]
            left_a[side * wide:(side + 1) * wide, pl.ds(at, chunk)] = kept.astype(jnp.bfloat16)

    whole = target_ref[...]
    high = whole.astype(jnp.bfloat16)
    rest = whole - high.astype(jnp.float32)
    middle = rest.astype(jnp.bfloat16)
    low = (rest - middle.astype(jnp.float32)).astype(jnp.bfloat16)
    for side in range(2):
        columns = g[side]
        parts = [
            jnp.dot(part, columns, preferred_element_type=jnp.float32)
            for part in (low, middle, high)
        ]
        rhs[0, :, side * wide:(side + 1) * wide] = (parts[0] + parts[1]) + parts[2]

    def rhs_copy(stage, device):
        return pltpu.make_async_remote_copy(
            src_ref=rhs.at[stage], dst_ref=rhs_recv.at[stage],
            send_sem=rhs_ss.at[stage], recv_sem=rhs_rs.at[stage],
            device_id=device, device_id_type=MESH,
        )

    rhs_copy(0, {"fold": mate}).start()
    rhs_copy(0, {"fold": mate}).wait()
    rhs[1] = rhs[0] + rhs_recv[0]
    rhs_copy(1, {"fold": across}).start()

    def scatter(unit):
        return pltpu.make_async_remote_copy(
            src_ref=rs_send.at[unit % 2], dst_ref=rs_recv.at[unit % SLOTS],
            send_sem=rs_ss.at[unit % 2], recv_sem=rs_rs.at[unit % SLOTS],
            device_id={"fold": mate}, device_id_type=MESH,
        )

    def cross(unit):
        return pltpu.make_async_remote_copy(
            src_ref=x_send.at[unit % 2], dst_ref=x_recv.at[unit % SLOTS],
            send_sem=x_ss.at[unit % 2], recv_sem=x_rs.at[unit % SLOTS],
            device_id={"fold": across}, device_id_type=MESH,
        )

    def share(unit):
        return pltpu.make_async_remote_copy(
            src_ref=ag_send.at[unit % 2], dst_ref=ag_recv.at[unit % SLOTS],
            send_sem=ag_ss.at[unit % 2], recv_sem=ag_rs.at[unit % SLOTS],
            device_id={"fold": mate}, device_id_type=MESH,
        )

    def store(unit):
        side, step = unit % 2, unit // 2
        owner = tile_at(place + tiles + (2 * side - 1) * step)
        column = pl.multiple_of(owner * block + side * wide, wide)
        return pltpu.make_async_copy(
            grams.at[unit % SLOTS], out_ref.at[:, :, pl.ds(column, wide)],
            out_sem.at[unit % SLOTS],
        )

    mine = pl.ds(pl.multiple_of(core * half, half), half)
    other = pl.ds(pl.multiple_of((1 - core) * half, half), half)

    def products(unit, rows):
        slot = unit % SLOTS
        columns = g[unit]
        both = jnp.dot(left[rows, :], columns, preferred_element_type=jnp.float32)
        first = jnp.dot(left_a[rows, :], columns, preferred_element_type=jnp.float32)
        grams[slot, 0, rows, :] = first.astype(jnp.bfloat16)
        grams[slot, 1, rows, :] = (both - first).astype(jnp.bfloat16)
        return both

    def turn(k, carry):
        @pl.when((k >= 1) & (k <= units - 2))
        def _():
            step, sub = (k + 1) // 2, (k + 1) % 2
            for side in range(2):
                hop(step - 1, side, sub).wait_recv()

                @pl.when(step < tiles - 1)
                def _():
                    hop(step, side, sub).start()

        @pl.when((k >= 4) & (k - 4 < units))
        def _():
            store(k - 4).wait()

        @pl.when((k >= 3) & (k - 3 < units))
        def _():
            unit = k - 3
            slot = unit % SLOTS
            share(unit).wait()

            def finish(rows, sums):
                total = sums.astype(jnp.float32)
                for held in range(2):
                    part = grams[slot, held, rows, :].astype(jnp.float32)
                    grams[slot, held, rows, :] = (total - part).astype(jnp.bfloat16)

            finish(mine, ag_send[unit % 2])
            finish(other, ag_recv[slot])

            @pl.when(unit < 2)
            def _():
                for piece in range(wide // 128):
                    rows = pl.ds(pl.multiple_of(unit * wide + piece * 128, 128), 128)
                    cols = slice(piece * 128, (piece + 1) * 128)
                    for held in range(2):
                        now = grams[slot, held, rows, cols].astype(jnp.float32)
                        grams[slot, held, rows, cols] = (now + pen_ref[rows, :]).astype(
                            jnp.bfloat16
                        )

            store(unit).start()

        @pl.when((k >= 2) & (k - 2 < units))
        def _():
            unit = k - 2
            cross(unit).wait()
            ag_send[unit % 2] = (
                x_send[unit % 2].astype(jnp.float32)
                + x_recv[unit % SLOTS].astype(jnp.float32)
            ).astype(jnp.bfloat16)
            share(unit).start()

        @pl.when((k >= 1) & (k - 1 < units))
        def _():
            unit = k - 1
            slot = unit % SLOTS
            scatter(unit).wait()
            own = grams[slot, 0, mine, :].astype(jnp.float32) + grams[
                slot, 1, mine, :
            ].astype(jnp.float32)
            x_send[unit % 2] = (own + rs_recv[slot].astype(jnp.float32)).astype(jnp.bfloat16)
            cross(unit).start()

        @pl.when(k < units)
        def _():
            rs_send[k % 2] = products(k, other).astype(jnp.bfloat16)
            scatter(k).start()
            products(k, mine)

        return carry

    lax.fori_loop(0, units + 4, turn, 0)

    rhs_copy(1, {"fold": across}).wait()
    sums = rhs[1] + rhs_recv[1]
    crhs_ref[...] = (sums[0:1] + sums[1:2]) - rhs[0]

    def drain(step, carry):
        for side in range(2):
            for sub in range(2):
                hop(step, side, sub).wait_send()
        return carry

    lax.fori_loop(0, tiles - 1, drain, 0)


def body(tiles, design, weights, response, fold_of, smoothing):
    depth, block = design.shape
    wide = block // 2
    half = block // 2
    slab_rows = depth // fold_of.shape[0]
    held = FOLDS // lax.axis_size("fold")
    first_fold = lax.axis_index("fold") * held
    root_w = jnp.sqrt(weights)
    rooted = (design.astype(jnp.float32) * root_w[:, None]).astype(jnp.bfloat16)
    target = root_w * response
    row_fold = jnp.repeat(fold_of - first_fold, slab_rows)
    mask = (row_fold == 0).astype(jnp.float32)[None, :]
    line = lax.broadcasted_iota(jnp.int32, (16, depth), 0)
    targets = jnp.where(line == row_fold[None, :], target[None, :], 0.0)
    term_row = jnp.repeat(smoothing, TERM)[:, None]
    pattern = jnp.tile(second_differences(TERM), (block // TERM, 2))
    spot = (lax.broadcasted_iota(jnp.int32, (block, 2 * TERM), 0) // TERM) % 2
    spot = spot == lax.broadcasted_iota(jnp.int32, (block, 2 * TERM), 1) // TERM
    pen = jnp.where(spot, term_row * pattern, 0.0)
    bf16, f32 = jnp.bfloat16, jnp.float32
    dma = pltpu.SemaphoreType.DMA
    vmem = pl.BlockSpec(memory_space=pltpu.VMEM)
    hbm = pl.BlockSpec(memory_space=pl.ANY)
    size = tiles * block
    compact, crhs = pl.pallas_call(
        functools.partial(kernel, tiles),
        out_shape=(
            jax.ShapeDtypeStruct((2, block, size), bf16),
            jax.ShapeDtypeStruct((16, block), f32),
        ),
        in_specs=[hbm, vmem, vmem, vmem],
        out_specs=(hbm, vmem),
        scratch_shapes=[
            pltpu.VMEM((2 * tiles, depth, wide), bf16),
            pltpu.VMEM((block, depth), bf16),
            pltpu.VMEM((block, depth), bf16),
            pltpu.VMEM((SLOTS, 2, block, wide), bf16),
            pltpu.VMEM((2, half, wide), bf16),
            pltpu.VMEM((SLOTS, half, wide), bf16),
            pltpu.VMEM((2, half, wide), bf16),
            pltpu.VMEM((SLOTS, half, wide), bf16),
            pltpu.VMEM((2, half, wide), bf16),
            pltpu.VMEM((SLOTS, half, wide), bf16),
            pltpu.VMEM((2, 16, block), f32),
            pltpu.VMEM((2, 16, block), f32),
            dma((2,)),
            dma((2 * tiles, 2)),
            dma((2 * tiles, 2)),
            dma((2,)),
            dma((SLOTS,)),
            dma((2,)),
            dma((SLOTS,)),
            dma((2,)),
            dma((SLOTS,)),
            dma((SLOTS,)),
            dma((2,)),
            dma((2,)),
        ],
        compiler_params=pltpu.CompilerParams(
            collective_id=0, has_side_effects=True, vmem_limit_bytes=63 * 2**20
        ),
        cost_estimate=pl.CostEstimate(
            flops=4 * depth * block * size, bytes_accessed=8 * block * size, transcendentals=0
        ),
    )(rooted, mask, targets, pen)
    return (compact.astype(f32), crhs[:2])


def solution(mesh):
    tiles = mesh.shape["tile"]
    in_specs = (P("fold", "tile"), P("fold"), P("fold"), P("fold"), P("tile"))
    out_specs = (P("fold", "tile", None), P("fold", "tile"))
    return jax.shard_map(
        functools.partial(body, tiles),
        mesh=mesh, in_specs=in_specs, out_specs=out_specs, check_vma=False,
    )
```

```python
import functools

import jax
import jax.numpy as jnp
from jax import lax
from jax.experimental import pallas as pl
from jax.experimental.pallas import tpu as pltpu
from jax.sharding import PartitionSpec as P

FOLDS = 8
TERM = 64
MESH = pl.DeviceIdType.MESH
SLOTS = 4


def second_differences(width):
    rows = lax.broadcasted_iota(jnp.int32, (width - 2, width), 0)
    cols = lax.broadcasted_iota(jnp.int32, (width - 2, width), 1)
    diffs = (
        jnp.where(cols == rows, 1.0, 0.0)
        + jnp.where(cols == rows + 1, -2.0, 0.0)
        + jnp.where(cols == rows + 2, 1.0, 0.0)
    )
    diffs = diffs.astype(jnp.float32)
    return jnp.dot(
        diffs.T, diffs, precision=lax.Precision.HIGHEST, preferred_element_type=jnp.float32
    )


def kernel(
    tiles, x_ref, mask_ref, target_ref, pen_ref, out_ref, crhs_ref,
    g, left, left_a, grams, rs_send, rs_recv, x_send, x_recv, ag_send, ag_recv,
    rhs, rhs_recv,
    in_sem, ring_send, ring_recv, rs_ss, rs_rs, x_ss, x_rs, ag_ss, ag_rs, out_sem,
    rhs_ss, rhs_rs,
):
    units = 2 * tiles
    depth, wide = g.shape[1], g.shape[2]
    block = 2 * wide
    half = block // 2
    sub_rows = depth // 2
    me = lax.axis_index("tile")
    fold = lax.axis_index("fold")
    core = fold % 2
    mate = fold + 1 - 2 * core
    across = (fold + 2) % 4
    place = (1 - me % 2) * (me // 2) + (me % 2) * (tiles - 1 - me // 2)

    def tile_at(position):
        position = position % tiles
        up = (position < tiles // 2).astype(jnp.int32)
        return up * (2 * position) + (1 - up) * (2 * (tiles - 1 - position) + 1)

    right = tile_at(place + 1)
    left_tile = tile_at(place + tiles - 1)
    neighbours = (right, left_tile)

    barrier = pltpu.get_barrier_semaphore()
    for device in ({"tile": right}, {"tile": left_tile}, {"fold": mate}, {"fold": across}):
        pl.semaphore_signal(barrier, inc=1, device_id=device, device_id_type=MESH)

    def load(side):
        return pltpu.make_async_copy(
            x_ref.at[:, pl.ds(side * wide, wide)], g.at[side], in_sem.at[side]
        )

    load(0).start()
    load(1).start()
    pl.semaphore_wait(barrier, 4)

    def hop(step, side, sub):
        rows = pl.ds(pl.multiple_of(sub * sub_rows, sub_rows), sub_rows)
        source, there = 2 * step + side, 2 * step + 2 + side
        return pltpu.make_async_remote_copy(
            src_ref=g.at[source, rows],
            dst_ref=g.at[there, rows],
            send_sem=ring_send.at[source, sub],
            recv_sem=ring_recv.at[there, sub],
            device_id={"tile": neighbours[side]},
            device_id_type=MESH,
        )

    for side in range(2):
        load(side).wait()
        for sub in range(2):
            hop(0, side, sub).start()

    chunk = 256
    for side in range(2):
        @pl.loop(0, depth // chunk)
        def _(i):
            at = pl.multiple_of(i * chunk, chunk)
            turned = g[side, pl.ds(at, chunk), :].T
            left[side * wide:(side + 1) * wide, pl.ds(at, chunk)] = turned
            kept = turned.astype(jnp.float32) * mask_ref[:, pl.ds(at, chunk)]
            left_a[side * wide:(side + 1) * wide, pl.ds(at, chunk)] = kept.astype(jnp.bfloat16)

    whole = target_ref[...]
    high = whole.astype(jnp.bfloat16)
    rest = whole - high.astype(jnp.float32)
    middle = rest.astype(jnp.bfloat16)
    low = (rest - middle.astype(jnp.float32)).astype(jnp.bfloat16)
    for side in range(2):
        columns = g[side]
        parts = [
            jnp.dot(part, columns, preferred_element_type=jnp.float32)
            for part in (low, middle, high)
        ]
        rhs[0, :, side * wide:(side + 1) * wide] = (parts[0] + parts[1]) + parts[2]

    def rhs_copy(stage, device):
        return pltpu.make_async_remote_copy(
            src_ref=rhs.at[stage], dst_ref=rhs_recv.at[stage],
            send_sem=rhs_ss.at[stage], recv_sem=rhs_rs.at[stage],
            device_id=device, device_id_type=MESH,
        )

    rhs_copy(0, {"fold": mate}).start()
    rhs_copy(0, {"fold": mate}).wait()
    rhs[1] = rhs[0] + rhs_recv[0]
    rhs_copy(1, {"fold": across}).start()

    def scatter(unit):
        return pltpu.make_async_remote_copy(
            src_ref=rs_send.at[unit % 2], dst_ref=rs_recv.at[unit % SLOTS],
            send_sem=rs_ss.at[unit % 2], recv_sem=rs_rs.at[unit % SLOTS],
            device_id={"fold": mate}, device_id_type=MESH,
        )

    def cross(unit):
        return pltpu.make_async_remote_copy(
            src_ref=x_send.at[unit % 2], dst_ref=x_recv.at[unit % SLOTS],
            send_sem=x_ss.at[unit % 2], recv_sem=x_rs.at[unit % SLOTS],
            device_id={"fold": across}, device_id_type=MESH,
        )

    def share(unit):
        return pltpu.make_async_remote_copy(
            src_ref=ag_send.at[unit % 2], dst_ref=ag_recv.at[unit % SLOTS],
            send_sem=ag_ss.at[unit % 2], recv_sem=ag_rs.at[unit % SLOTS],
            device_id={"fold": mate}, device_id_type=MESH,
        )

    def store(unit):
        side, step = unit % 2, unit // 2
        owner = tile_at(place + tiles + (2 * side - 1) * step)
        column = pl.multiple_of(owner * block + side * wide, wide)
        return pltpu.make_async_copy(
            grams.at[unit % SLOTS], out_ref.at[:, :, pl.ds(column, wide)],
            out_sem.at[unit % SLOTS],
        )

    mine = pl.ds(pl.multiple_of(core * half, half), half)
    other = pl.ds(pl.multiple_of((1 - core) * half, half), half)

    def products(unit, rows):
        slot = unit % SLOTS
        columns = g[unit]
        both = jnp.dot(left[rows, :], columns, preferred_element_type=jnp.float32)
        first = jnp.dot(left_a[rows, :], columns, preferred_element_type=jnp.float32)
        grams[slot, 0, rows, :] = first.astype(jnp.bfloat16)
        grams[slot, 1, rows, :] = (both - first).astype(jnp.bfloat16)
        return both

    def turn(k, carry):
        @pl.when((k >= 1) & (k <= units - 2))
        def _():
            step, sub = (k + 1) // 2, (k + 1) % 2
            for side in range(2):
                hop(step - 1, side, sub).wait_recv()

                @pl.when(step < tiles - 1)
                def _():
                    hop(step, side, sub).start()

        @pl.when((k >= 4) & (k - 4 < units))
        def _():
            store(k - 4).wait()

        @pl.when((k >= 1) & (k - 1 < units))
        def _():
            unit = k - 1
            slot = unit % SLOTS
            scatter(unit).wait()
            own = grams[slot, 0, mine, :].astype(jnp.float32) + grams[
                slot, 1, mine, :
            ].astype(jnp.float32)
            x_send[unit % 2] = (own + rs_recv[slot].astype(jnp.float32)).astype(jnp.bfloat16)
            cross(unit).start()

        @pl.when(k < units)
        def _():
            rs_send[k % 2] = products(k, other).astype(jnp.bfloat16)
            scatter(k).start()
            products(k, mine)

        @pl.when((k >= 2) & (k - 2 < units))
        def _():
            unit = k - 2
            cross(unit).wait()
            ag_send[unit % 2] = (
                x_send[unit % 2].astype(jnp.float32)
                + x_recv[unit % SLOTS].astype(jnp.float32)
            ).astype(jnp.bfloat16)
            share(unit).start()

        @pl.when((k >= 3) & (k - 3 < units))
        def _():
            unit = k - 3
            slot = unit % SLOTS
            share(unit).wait()

            def finish(rows, sums):
                total = sums.astype(jnp.float32)
                for held in range(2):
                    part = grams[slot, held, rows, :].astype(jnp.float32)
                    grams[slot, held, rows, :] = (total - part).astype(jnp.bfloat16)

            finish(mine, ag_send[unit % 2])
            finish(other, ag_recv[slot])

            @pl.when(unit < 2)
            def _():
                for piece in range(wide // 128):
                    rows = pl.ds(pl.multiple_of(unit * wide + piece * 128, 128), 128)
                    cols = slice(piece * 128, (piece + 1) * 128)
                    for held in range(2):
                        now = grams[slot, held, rows, cols].astype(jnp.float32)
                        grams[slot, held, rows, cols] = (now + pen_ref[rows, :]).astype(
                            jnp.bfloat16
                        )

            store(unit).start()

        return carry

    lax.fori_loop(0, units + 4, turn, 0)

    rhs_copy(1, {"fold": across}).wait()
    sums = rhs[1] + rhs_recv[1]
    crhs_ref[...] = (sums[0:1] + sums[1:2]) - rhs[0]

    def drain(step, carry):
        for side in range(2):
            for sub in range(2):
                hop(step, side, sub).wait_send()
        return carry

    lax.fori_loop(0, tiles - 1, drain, 0)


def body(tiles, design, weights, response, fold_of, smoothing):
    depth, block = design.shape
    wide = block // 2
    half = block // 2
    slab_rows = depth // fold_of.shape[0]
    held = FOLDS // lax.axis_size("fold")
    first_fold = lax.axis_index("fold") * held
    root_w = jnp.sqrt(weights)
    rooted = (design.astype(jnp.float32) * root_w[:, None]).astype(jnp.bfloat16)
    target = root_w * response
    row_fold = jnp.repeat(fold_of - first_fold, slab_rows)
    mask = (row_fold == 0).astype(jnp.float32)[None, :]
    line = lax.broadcasted_iota(jnp.int32, (16, depth), 0)
    targets = jnp.where(line == row_fold[None, :], target[None, :], 0.0)
    term_row = jnp.repeat(smoothing, TERM)[:, None]
    pattern = jnp.tile(second_differences(TERM), (block // TERM, 2))
    spot = (lax.broadcasted_iota(jnp.int32, (block, 2 * TERM), 0) // TERM) % 2
    spot = spot == lax.broadcasted_iota(jnp.int32, (block, 2 * TERM), 1) // TERM
    pen = jnp.where(spot, term_row * pattern, 0.0)
    bf16, f32 = jnp.bfloat16, jnp.float32
    dma = pltpu.SemaphoreType.DMA
    vmem = pl.BlockSpec(memory_space=pltpu.VMEM)
    hbm = pl.BlockSpec(memory_space=pl.ANY)
    size = tiles * block
    compact, crhs = pl.pallas_call(
        functools.partial(kernel, tiles),
        out_shape=(
            jax.ShapeDtypeStruct((2, block, size), bf16),
            jax.ShapeDtypeStruct((16, block), f32),
        ),
        in_specs=[hbm, vmem, vmem, vmem],
        out_specs=(hbm, vmem),
        scratch_shapes=[
            pltpu.VMEM((2 * tiles, depth, wide), bf16),
            pltpu.VMEM((block, depth), bf16),
            pltpu.VMEM((block, depth), bf16),
            pltpu.VMEM((SLOTS, 2, block, wide), bf16),
            pltpu.VMEM((2, half, wide), bf16),
            pltpu.VMEM((SLOTS, half, wide), bf16),
            pltpu.VMEM((2, half, wide), bf16),
            pltpu.VMEM((SLOTS, half, wide), bf16),
            pltpu.VMEM((2, half, wide), bf16),
            pltpu.VMEM((SLOTS, half, wide), bf16),
            pltpu.VMEM((2, 16, block), f32),
            pltpu.VMEM((2, 16, block), f32),
            dma((2,)),
            dma((2 * tiles, 2)),
            dma((2 * tiles, 2)),
            dma((2,)),
            dma((SLOTS,)),
            dma((2,)),
            dma((SLOTS,)),
            dma((2,)),
            dma((SLOTS,)),
            dma((SLOTS,)),
            dma((2,)),
            dma((2,)),
        ],
        compiler_params=pltpu.CompilerParams(
            collective_id=0, has_side_effects=True, vmem_limit_bytes=63 * 2**20
        ),
        cost_estimate=pl.CostEstimate(
            flops=4 * depth * block * size, bytes_accessed=8 * block * size, transcendentals=0
        ),
    )(rooted, mask, targets, pen)
    return (compact.astype(f32), crhs[:2])


def solution(mesh):
    tiles = mesh.shape["tile"]
    in_specs = (P("fold", "tile"), P("fold"), P("fold"), P("fold"), P("tile"))
    out_specs = (P("fold", "tile", None), P("fold", "tile"))
    return jax.shard_map(
        functools.partial(body, tiles),
        mesh=mesh, in_specs=in_specs, out_specs=out_specs, check_vma=False,
    )
```
